32 devices in a mesh: dp: 4 (over x, core), row: 4 (over z), col: 2 (over y).
Axes of the slice: x: 2, y: 2, z: 4, core: 2. Of those that a mesh axis runs over, the one named last changes fastest.
Arguments:
- inputs: bfloat16 [2048, 8192], P(('dp', 'col'), 'row'), may hold values from -6 to 6
- w_in: bfloat16 [8192, 16384], P('row', 'col'), may hold values from -0.0625 to 0.0625
- w_out: bfloat16 [16384, 8192], P('col', 'row'), may hold values from -0.046875 to 0.046875
- grad_outputs: bfloat16 [2048, 8192], P(('dp', 'col'), 'row'), may hold values from -6 to 6
Outputs:
- outputs: bfloat16 [2048, 8192], P(('dp', 'col'), 'row')
- grad_inputs: bfloat16 [2048, 8192], P(('dp', 'col'), 'row')
- grad_w_in: bfloat16 [8192, 16384], P(('row', 'dp'), 'col')
- grad_w_out: bfloat16 [16384, 8192], P('col', ('row', 'dp'))
The draws below stay inside these ranges and needn't reach their ends.
All inputs are finite; a program needn't handle non-finite values.
Results may differ from the reference program's by a relative error of at most 0.024.
Values may be sent and summed in bfloat16 or wider, within the bound.
A program may use at most 320 MiB of HBM per device.

```python
import jax
import jax.numpy as jnp
from jax import lax

D = 8192
FF = 16384
TOKENS = 2048


def steps_of(key, extent, split, least, largest):
    factor_of = 1.0
    for axis_at, parts in split:
        steps = jax.random.uniform(jax.random.fold_in(jax.random.fold_in(key, 6), axis_at), (parts,), jnp.float32, least / len(split), largest / len(split))
        factor_of = factor_of * jnp.repeat(jnp.exp(steps), extent[axis_at] // parts).reshape((-1,) + (1,) * (len(extent) - 1 - axis_at))
    return factor_of


def noise(rng, extent, deviation, bound, split=(), kind=jnp.bfloat16):
    result = jax.random.normal(rng, extent, jnp.float32) * deviation
    if len(split) > 0:
        result = steps_of(rng, extent, split, -0.22, 0.18) * result
    return jnp.clip(result, min=-bound, max=bound).astype(kind)


def setup_inputs(seed: int = 0) -> dict:
    splits = jax.random.split(jax.random.key(seed), 5)
    return {
        "inputs": noise(splits[0], (TOKENS, D), 1.0, 6.0, ((0, 8), (1, 4))),
        "w_in": noise(splits[1], (D, FF), D ** -0.5, 0.0625, ((0, 4), (1, 2))),
        "w_out": noise(splits[2], (FF, D), FF ** -0.5, 0.046875, ((0, 2), (1, 4))),
        "grad_outputs": noise(splits[3], (TOKENS, D), 1.0, 6.0, ((0, 8), (1, 4))),
    }


def gelu_fn(values):
    return jax.nn.gelu(values, approximate=True)

def contract(left, right, left_dim, right_dim):
    return lax.dot_general(left, right, (((left_dim,), (right_dim,)), ((), ())), preferred_element_type=jnp.float32)

def reference(inputs, w_in, w_out, grad_outputs):
    preact = jnp.dot(inputs, w_in, preferred_element_type=jnp.float32)
    activated = gelu_fn(preact).astype(jnp.bfloat16)
    outputs = (inputs.astype(jnp.float32) + jnp.dot(activated, w_out, preferred_element_type=jnp.float32)).astype(jnp.bfloat16)
    grad_activated = contract(grad_outputs, w_out, 1, 1)
    grad_preact = jax.vjp(gelu_fn, preact)[1](grad_activated)[0].astype(jnp.bfloat16)
    grad_inputs = (grad_outputs.astype(jnp.float32) + contract(grad_preact, w_in, 1, 1)).astype(jnp.bfloat16)
    grad_w_in = contract(inputs, grad_preact, 0, 0).astype(jnp.bfloat16)
    grad_w_out = contract(activated, grad_outputs, 0, 0).astype(jnp.bfloat16)
    return (outputs, grad_inputs, grad_w_in, grad_w_out)
```

```python
import jax
import jax.numpy as jnp
from jax import lax
from jax.sharding import PartitionSpec as P

PARTS = 2


def gelu_fn(values):
    return jax.nn.gelu(values, approximate=True)


def contract(left, right, left_dim, right_dim):
    return lax.dot_general(
        left, right, (((left_dim,), (right_dim,)), ((), ())), preferred_element_type=jnp.float32
    )


def plus(left, right):
    return (left.astype(jnp.float32) + right.astype(jnp.float32)).astype(jnp.bfloat16)


def take(array, index, dim):
    return lax.dynamic_index_in_dim(array, index, dim, keepdims=True)


def swap(array, axis, size, mask):
    return lax.ppermute(array, axis, [(k, k ^ mask) for k in range(size)])


def sum_over_row(part, n):
    me = lax.axis_index("row")
    right = left = None
    for t in range(n - 1):
        block = take(part, jnp.clip(n - 1 - t + me, 0, n - 1), 0)
        block = block if right is None else plus(block, right)
        right = lax.ppermute(block, "row", [(k, k + 1) for k in range(t + 1)])
        block = take(part, jnp.clip(t - n + 1 + me, 0, n - 1), 0)
        block = block if left is None else plus(block, left)
        left = lax.ppermute(block, "row", [(k, k - 1) for k in range(n - 1, n - 2 - t, -1)])
    return (
        take(part, me, 0).astype(jnp.float32) + right.astype(jnp.float32) + left.astype(jnp.float32)
    )


def gather_over_row(own, n):
    me = lax.axis_index("row")
    right = left = own
    rights, lefts = [], []
    for t in range(n - 1):
        right = lax.ppermute(right, "row", [(k, k + 1) for k in range(t, n - 1)])
        left = lax.ppermute(left, "row", [(k, k - 1) for k in range(n - 1 - t, 0, -1)])
        rights.append(right)
        lefts.append(left)
    whole = jnp.zeros((n,) + own.shape[1:], own.dtype)
    whole = lax.dynamic_update_slice_in_dim(whole, own, me, 0)
    for t in range(n - 1):
        block = jnp.where(me >= t + 1, rights[t], lefts[n - 2 - t])
        whole = lax.dynamic_update_slice_in_dim(whole, block, lax.rem(me + n - 1 - t, n), 0)
    return whole


def solution(mesh):
    n_dp, n_row, n_col = mesh.shape["dp"], mesh.shape["row"], mesh.shape["col"]
    dp_bits, col_bits = n_dp.bit_length() - 1, n_col.bit_length() - 1
    digits = [("dp", n_dp, 1 << b) for b in reversed(range(dp_bits))]
    digits += [("col", n_col, 1 << b) for b in reversed(range(col_bits))]
    core = [dp_bits - 1]
    far = list(range(dp_bits - 1))
    cols = list(range(dp_bits, dp_bits + col_bits))

    def digit(d):
        axis, _, weight = digits[d]
        return lax.rem(lax.axis_index(axis) // weight, 2)

    def gather_tokens(block, order):
        array = block.reshape((1,) * len(digits) + block.shape)
        for d in order:
            axis, size, weight = digits[d]
            other = swap(array, axis, size, weight)
            low = digit(d) == 0
            array = jnp.concatenate(
                [jnp.where(low, array, other), jnp.where(low, other, array)], axis=d
            )
        return array.reshape(-1, block.shape[-1])

    def scatter_tokens(part, order):
        array = part.reshape((2,) * len(digits) + (-1, part.shape[-1]))
        for at, d in enumerate(order):
            axis, size, weight = digits[d]
            other = swap(take(array, 1 - digit(d), d), axis, size, weight)
            kept = take(array, digit(d), d)
            if at == len(order) - 1:
                array = kept.astype(jnp.float32) + other.astype(jnp.float32)
            else:
                array = plus(kept, other)
        return array.reshape(-1, part.shape[-1])

    def shards(inputs, w_in, w_out, grad_outputs):
        dp = lax.axis_index("dp")
        model, hidden = w_in.shape
        share = hidden // n_dp
        width = share // PARTS
        piece = model // n_dp

        all_in = gather_tokens(inputs, cols + far + core)
        all_cot = gather_tokens(grad_outputs, far + cols + core)
        tokens = all_in.shape[0]
        blocks = (n_row, tokens // n_row, width)
        grad_w_in = jnp.zeros((piece, hidden), jnp.bfloat16)
        grad_w_out = jnp.zeros((hidden, piece), jnp.bfloat16)
        out_part = input_part = None
        for h in range(PARTS):
            first = dp * share + h * width
            w_in_h = lax.dynamic_slice_in_dim(w_in, first, width, 1)
            w_out_h = lax.dynamic_slice_in_dim(w_out, first, width, 0)
            part = contract(all_in, w_in_h, 1, 0).astype(jnp.bfloat16)
            preact = sum_over_row(part.reshape(blocks), n_row)
            activated = gelu_fn(preact).astype(jnp.bfloat16)
            part = contract(all_cot, w_out_h, 1, 1).astype(jnp.bfloat16)
            grad_activated = sum_over_row(part.reshape(blocks), n_row)
            grad_preact = jax.vjp(gelu_fn, preact)[1](grad_activated)[0].astype(jnp.bfloat16)
            all_act = gather_over_row(activated, n_row).reshape(tokens, width)
            all_grad = gather_over_row(grad_preact, n_row).reshape(tokens, width)

            term = contract(all_act, w_out_h, 1, 0)
            out_part = term if out_part is None else out_part + term
            term = contract(all_grad, w_in_h, 1, 1)
            input_part = term if input_part is None else input_part + term

            whole_out = contract(all_act, all_cot, 0, 0).astype(jnp.bfloat16)
            whole_in = contract(all_in, all_grad, 0, 0).astype(jnp.bfloat16)
            for mask in range(n_dp):
                peer = dp ^ mask
                place = peer * share + h * width
                block = lax.dynamic_slice_in_dim(whole_out, peer * piece, piece, 1)
                block = swap(block, "dp", n_dp, mask) if mask else block
                grad_w_out = lax.dynamic_update_slice_in_dim(grad_w_out, block, place, 0)
                block = lax.dynamic_slice_in_dim(whole_in, peer * piece, piece, 0)
                block = swap(block, "dp", n_dp, mask) if mask else block
                grad_w_in = lax.dynamic_update_slice_in_dim(grad_w_in, block, place, 1)
        out_sum = scatter_tokens(out_part.astype(jnp.bfloat16), core + far + cols)
        outputs = (inputs.astype(jnp.float32) + out_sum).astype(jnp.bfloat16)
        input_sum = scatter_tokens(input_part.astype(jnp.bfloat16), core + cols + far)
        grad_inputs = (grad_outputs.astype(jnp.float32) + input_sum).astype(jnp.bfloat16)
        return (outputs, grad_inputs, grad_w_in, grad_w_out)

    return jax.shard_map(
        shards,
        mesh=mesh,
        in_specs=(
            P(("dp", "col"), "row"),
            P("row", "col"),
            P("col", "row"),
            P(("dp", "col"), "row"),
        ),
        out_specs=(
            P(("dp", "col"), "row"),
            P(("dp", "col"), "row"),
            P(("row", "dp"), "col"),
            P("col", ("row", "dp")),
        ),
        check_vma=False,
    )
```

```python
import jax
import jax.numpy as jnp
from jax import lax
from jax.sharding import PartitionSpec as P

PARTS = 2


def gelu_fn(values):
    return jax.nn.gelu(values, approximate=True)


def contract(left, right, left_dim, right_dim):
    return lax.dot_general(
        left, right, (((left_dim,), (right_dim,)), ((), ())), preferred_element_type=jnp.float32
    )


def swap(array, axis, size, mask):
    return lax.ppermute(array, axis, [(k, k ^ mask) for k in range(size)])


def sum_over_row(part):
    return lax.psum_scatter(part, "row", scatter_dimension=0, tiled=True)


def gather_over_row(own, n):
    me = lax.axis_index("row")
    right = left = own
    rights, lefts = [], []
    for t in range(n - 1):
        right = lax.ppermute(right, "row", [(k, k + 1) for k in range(t, n - 1)])
        left = lax.ppermute(left, "row", [(k, k - 1) for k in range(n - 1 - t, 0, -1)])
        rights.append(right)
        lefts.append(left)
    whole = jnp.zeros((n,) + own.shape[1:], own.dtype)
    whole = lax.dynamic_update_slice_in_dim(whole, own, me, 0)
    for t in range(n - 1):
        block = jnp.where(me >= t + 1, rights[t], lefts[n - 2 - t])
        whole = lax.dynamic_update_slice_in_dim(whole, block, lax.rem(me + n - 1 - t, n), 0)
    return whole


def solution(mesh):
    n_dp, n_row, n_col = mesh.shape["dp"], mesh.shape["row"], mesh.shape["col"]
    dp_bits, col_bits = n_dp.bit_length() - 1, n_col.bit_length() - 1
    digits = [("dp", n_dp, 1 << b) for b in reversed(range(dp_bits))]
    digits += [("col", n_col, 1 << b) for b in reversed(range(col_bits))]
    core = [dp_bits - 1]
    far = list(range(dp_bits - 1))
    cols = list(range(dp_bits, dp_bits + col_bits))

    def digit(d):
        axis, _, weight = digits[d]
        return lax.rem(lax.axis_index(axis) // weight, 2)

    def gather_tokens(block, order):
        array = block.reshape((1,) * len(digits) + block.shape)
        for d in order:
            axis, size, weight = digits[d]
            other = swap(array, axis, size, weight)
            low = digit(d) == 0
            array = jnp.concatenate(
                [jnp.where(low, array, other), jnp.where(low, other, array)], axis=d
            )
        return array.reshape(-1, block.shape[-1])

    def scatter_tokens(part):
        return lax.psum_scatter(
            part.astype(jnp.bfloat16), ("dp", "col"), scatter_dimension=0, tiled=True
        ).astype(jnp.float32)

    def shards(inputs, w_in, w_out, grad_outputs):
        dp = lax.axis_index("dp")
        model, hidden = w_in.shape
        share = hidden // n_dp
        width = share // PARTS
        piece = model // n_dp

        all_in = lax.all_gather(inputs, ("dp", "col"), axis=0, tiled=True)
        all_cot = gather_tokens(grad_outputs, far + cols + core)
        tokens = all_in.shape[0]

        def blocks_of_peers(whole, dim):
            return [
                lax.dynamic_slice_in_dim(whole, (dp ^ mask) * piece, piece, dim)
                for mask in range(n_dp)
            ]

        def exchange(blocks):
            return [
                swap(block, "dp", n_dp, mask) if mask else block
                for mask, block in enumerate(blocks)
            ]

        firsts = [dp * share + h * width for h in range(PARTS)]
        w_ins = [lax.dynamic_slice_in_dim(w_in, first, width, 1) for first in firsts]
        w_outs = [lax.dynamic_slice_in_dim(w_out, first, width, 0) for first in firsts]

        units = [(back, h) for h in range(PARTS) for back in range(2)]
        parts = [
            contract(all_cot, w_outs[h], 1, 1) if back else contract(all_in, w_ins[h], 1, 0)
            for back, h in units
        ]
        parts = [part.astype(jnp.bfloat16) for part in parts]
        early = [sum_over_row(part) for part in parts[:2]]
        held = lax.optimization_barrier((early[0], *parts[2:]))
        sums = [held[0], early[1]] + [sum_over_row(part) for part in held[1:]]

        totals = [None, None]
        received = {}

        def products(u, every):
            back, h = units[u]
            if back:
                blocks = blocks_of_peers(contract(all_in, every, 0, 0).astype(jnp.bfloat16), 0)
                term = contract(every, w_ins[h], 1, 1)
            else:
                blocks = blocks_of_peers(contract(every, all_cot, 0, 0).astype(jnp.bfloat16), 1)
                term = contract(every, w_outs[h], 1, 0)
            received[units[u]] = exchange(blocks)
            totals[back] = term if totals[back] is None else totals[back] + term

        preact = every = None
        for u, (back, h) in enumerate(units):
            total = sums[u]
            if u >= 1:
                total, every = lax.optimization_barrier((total, every))
            if u >= 2:
                held = (total, every, received[units[u - 2]], totals[units[u - 2][0]])
                total, every, received[units[u - 2]], totals[units[u - 2][0]] = (
                    lax.optimization_barrier(held)
                )
            if u >= 1:
                products(u - 1, every)
            total = total.astype(jnp.float32)
            if back:
                own = jax.vjp(gelu_fn, preact)[1](total)[0].astype(jnp.bfloat16)
            else:
                preact = total
                own = gelu_fn(preact).astype(jnp.bfloat16)
            every = gather_over_row(own[None], n_row).reshape(tokens, width)
        last = len(units) - 1
        out_sum = scatter_tokens(totals[0])
        every, received[units[last - 1]] = lax.optimization_barrier(
            (every, received[units[last - 1]])
        )
        products(last, every)
        out_sum, input_total = lax.optimization_barrier((out_sum, totals[1].astype(jnp.bfloat16)))
        input_sum = scatter_tokens(input_total)

        grad_w_in = jnp.zeros((piece, hidden), jnp.bfloat16)
        grad_w_out = jnp.zeros((hidden, piece), jnp.bfloat16)
        for h in range(PARTS):
            for mask in range(n_dp):
                place = (dp ^ mask) * share + h * width
                grad_w_out = lax.dynamic_update_slice_in_dim(
                    grad_w_out, received[0, h][mask], place, 0
                )
                grad_w_in = lax.dynamic_update_slice_in_dim(grad_w_in, received[1, h][mask], place, 1)
        outputs = inputs.astype(jnp.float32) + out_sum
        grad_inputs = grad_outputs.astype(jnp.float32) + input_sum
        return (
            outputs.astype(jnp.bfloat16),
            grad_inputs.astype(jnp.bfloat16),
            grad_w_in,
            grad_w_out,
        )

    return jax.shard_map(
        shards,
        mesh=mesh,
        in_specs=(
            P(("dp", "col"), "row"),
            P("row", "col"),
            P("col", "row"),
            P(("dp", "col"), "row"),
        ),
        out_specs=(
            P(("dp", "col"), "row"),
            P(("dp", "col"), "row"),
            P(("row", "dp"), "col"),
            P("col", ("row", "dp")),
        ),
        check_vma=False,
    )
```

```python
import jax
import jax.numpy as jnp
from jax import lax
from jax.sharding import PartitionSpec as P

PARTS = 2


def gelu_fn(values):
    return jax.nn.gelu(values, approximate=True)


def contract(left, right, left_dim, right_dim):
    return lax.dot_general(
        left, right, (((left_dim,), (right_dim,)), ((), ())), preferred_element_type=jnp.float32
    )


def plus(left, right):
    return (left.astype(jnp.float32) + right.astype(jnp.float32)).astype(jnp.bfloat16)


def take(array, index, dim):
    return lax.dynamic_index_in_dim(array, index, dim, keepdims=True)


def swap(array, axis, size, mask):
    return lax.ppermute(array, axis, [(k, k ^ mask) for k in range(size)])


def sum_over_row(part, n):
    me = lax.axis_index("row")
    right = left = None
    for t in range(n - 1):
        block = take(part, jnp.clip(n - 1 - t + me, 0, n - 1), 0)
        block = block if right is None else plus(block, right)
        right = lax.ppermute(block, "row", [(k, k + 1) for k in range(t + 1)])
        block = take(part, jnp.clip(t - n + 1 + me, 0, n - 1), 0)
        block = block if left is None else plus(block, left)
        left = lax.ppermute(block, "row", [(k, k - 1) for k in range(n - 1, n - 2 - t, -1)])
    return (
        take(part, me, 0).astype(jnp.float32) + right.astype(jnp.float32) + left.astype(jnp.float32)
    )


def gather_over_row(own, n, whole, column):
    me = lax.axis_index("row")
    right = left = own
    rights, lefts = [], []
    for t in range(n - 1):
        right = lax.ppermute(right, "row", [(k, k + 1) for k in range(t, n - 1)])
        left = lax.ppermute(left, "row", [(k, k - 1) for k in range(n - 1 - t, 0, -1)])
        rights.append(right)
        lefts.append(left)
    whole = lax.dynamic_update_slice(whole, own, (me, 0, column))
    for t in range(n - 1):
        block = jnp.where(me >= t + 1, rights[t], lefts[n - 2 - t])
        whole = lax.dynamic_update_slice(whole, block, (lax.rem(me + n - 1 - t, n), 0, column))
    return whole


def solution(mesh):
    n_dp, n_row, n_col = mesh.shape["dp"], mesh.shape["row"], mesh.shape["col"]
    dp_bits, col_bits = n_dp.bit_length() - 1, n_col.bit_length() - 1
    digits = [("dp", n_dp, 1 << b) for b in reversed(range(dp_bits))]
    digits += [("col", n_col, 1 << b) for b in reversed(range(col_bits))]
    core = [dp_bits - 1]
    far = list(range(dp_bits - 1))
    cols = list(range(dp_bits, dp_bits + col_bits))

    def digit(d):
        axis, _, weight = digits[d]
        return lax.rem(lax.axis_index(axis) // weight, 2)

    def gather_tokens(block, order):
        array = block.reshape((1,) * len(digits) + block.shape)
        for d in order:
            axis, size, weight = digits[d]
            other = swap(array, axis, size, weight)
            low = digit(d) == 0
            array = jnp.concatenate(
                [jnp.where(low, array, other), jnp.where(low, other, array)], axis=d
            )
        return array.reshape(-1, block.shape[-1])

    def scatter_tokens(part, order):
        array = part.reshape((2,) * len(digits) + (-1, part.shape[-1]))
        for at, d in enumerate(order):
            axis, size, weight = digits[d]
            other = swap(take(array, 1 - digit(d), d), axis, size, weight)
            kept = take(array, digit(d), d)
            if at == len(order) - 1:
                array = kept.astype(jnp.float32) + other.astype(jnp.float32)
            else:
                array = plus(kept, other)
        return array.reshape(-1, part.shape[-1])

    def shards(inputs, w_in, w_out, grad_outputs):
        dp = lax.axis_index("dp")
        model, hidden = w_in.shape
        share = hidden // n_dp
        width = share // PARTS
        piece = model // n_dp

        all_in = lax.all_gather(inputs, ("dp", "col"), axis=0, tiled=True)
        all_cot = gather_tokens(grad_outputs, far + cols + core)
        tokens = all_in.shape[0]

        def blocks_of_peers(whole, dim):
            return [
                lax.dynamic_slice_in_dim(whole, (dp ^ mask) * piece, piece, dim)
                for mask in range(n_dp)
            ]

        def exchange(blocks):
            return [
                swap(block, "dp", n_dp, mask) if mask else block
                for mask, block in enumerate(blocks)
            ]

        firsts = [dp * share + h * width for h in range(PARTS)]
        w_ins = [lax.dynamic_slice_in_dim(w_in, first, width, 1) for first in firsts]
        w_outs = [lax.dynamic_slice_in_dim(w_out, first, width, 0) for first in firsts]

        lines = (n_row, tokens // n_row)

        def part_of(left, weights, dim):
            part = contract(left, weights, 1, dim).astype(jnp.bfloat16)
            return part.reshape(lines + (width,))

        def gather(owns):
            whole = jnp.zeros(lines + (share,), jnp.bfloat16)
            for h, own in enumerate(owns):
                whole = gather_over_row(own, n_row, whole, h * width)
            return whole.reshape(tokens, share)

        preacts = [sum_over_row(part_of(all_in, w_h, 0), n_row) for w_h in w_ins]
        parts = [part_of(all_cot, w_h, 1) for w_h in w_outs]
        for h in range(PARTS):
            preacts[h], parts[h] = lax.optimization_barrier((preacts[h], parts[h]))
        all_act = gather([gelu_fn(preact).astype(jnp.bfloat16) for preact in preacts])
        grads = [sum_over_row(part, n_row) for part in parts]
        grads, all_act = lax.optimization_barrier((grads, all_act))
        owns = [
            jax.vjp(gelu_fn, preact)[1](grad)[0].astype(jnp.bfloat16)
            for preact, grad in zip(preacts, grads)
        ]
        whole_out = contract(all_act, all_cot, 0, 0).astype(jnp.bfloat16)
        owns[-1], whole_out = lax.optimization_barrier((owns[-1], whole_out))
        all_grad = gather(owns)
        w_in_own = lax.dynamic_slice_in_dim(w_in, dp * share, share, 1)
        w_out_own = lax.dynamic_slice_in_dim(w_out, dp * share, share, 0)
        from_peers_out = exchange(blocks_of_peers(whole_out, 1))
        out_part = contract(all_act, w_out_own, 1, 0).astype(jnp.bfloat16)
        out_sum = scatter_tokens(out_part, core + far + cols)
        all_grad, from_peers_out, out_sum = lax.optimization_barrier(
            (all_grad, from_peers_out, out_sum)
        )
        whole_in = contract(all_in, all_grad, 0, 0).astype(jnp.bfloat16)
        from_peers_in = exchange(blocks_of_peers(whole_in, 0))
        input_part = contract(all_grad, w_in_own, 1, 1).astype(jnp.bfloat16)
        input_sum = scatter_tokens(input_part, core + cols + far)

        grad_w_in = jnp.zeros((piece, hidden), jnp.bfloat16)
        grad_w_out = jnp.zeros((hidden, piece), jnp.bfloat16)
        for mask in range(n_dp):
            place = (dp ^ mask) * share
            grad_w_out = lax.dynamic_update_slice_in_dim(grad_w_out, from_peers_out[mask], place, 0)
            grad_w_in = lax.dynamic_update_slice_in_dim(grad_w_in, from_peers_in[mask], place, 1)
        outputs = inputs.astype(jnp.float32) + out_sum
        grad_inputs = grad_outputs.astype(jnp.float32) + input_sum
        return (
            outputs.astype(jnp.bfloat16),
            grad_inputs.astype(jnp.bfloat16),
            grad_w_in,
            grad_w_out,
        )

    return jax.shard_map(
        shards,
        mesh=mesh,
        in_specs=(
            P(("dp", "col"), "row"),
            P("row", "col"),
            P("col", "row"),
            P(("dp", "col"), "row"),
        ),
        out_specs=(
            P(("dp", "col"), "row"),
            P(("dp", "col"), "row"),
            P(("row", "dp"), "col"),
            P("col", ("row", "dp")),
        ),
        check_vma=False,
    )
```
